32 devices in a mesh: member: 4 (over z), region: 8 (over y, x, core).
Axes of the slice: x: 2, y: 2, z: 4, core: 2. Of those that a mesh axis runs over, the one named last changes fastest.
Arguments:
- ensemble: bfloat16 [256, 256, 512], P(('member', 'region')), may hold values from -6 to 6
- obs_site: int32 [256, 2048], P(('member', 'region')), may hold values from 0 to 511
- obs_blocks: int32 [256], P(('member', 'region')), may hold values from 1 to 16
- obs_precision: bfloat16 [256, 2048], P(('member', 'region')), may hold values from 0.049804688 to 1
- obs_innovation: bfloat16 [256, 2048], P(('member', 'region')), may hold values from -6 to 6
Outputs:
- analysis: bfloat16 [256, 256, 512], P(('member', 'region'))
The draws below stay inside these ranges and needn't reach their ends.
Inputs may be any that keep to these rules, and one draw needn't show every extreme that they name: Only the first obs_blocks[p] blocks of 128 observations of patch p are used.
All inputs are finite; a program needn't handle non-finite values.
Results may differ from the reference program's by a relative error of at most 0.0062.
Values may be sent and summed in bfloat16 or wider, within the bound.
No kernel may reach another device: no remote copies, remote signals or barrier semaphores. Data moves between devices by JAX's collectives and lax.ppermute only.
A program may use at most 64 MiB of HBM per device.

```python
import math
import jax
import jax.numpy as jnp
from jax import lax

K = 256
S = 512
OB = 128
BMAX = 16
ITERS = 6
P_SIZE = 256


def with_ends(drawn, own_key, least, top_value):
    spot = [jax.random.randint(jax.random.fold_in(own_key, axis), (), 0, length) for axis, length in enumerate(drawn.shape)]
    main_axis = drawn.shape.index(max(drawn.shape))
    neighbour = spot[:main_axis] + [(spot[main_axis] + 1) % drawn.shape[main_axis]] + spot[main_axis + 1:]
    return drawn.at[tuple(spot)].set(least).at[tuple(neighbour)].set(top_value)


def steps_of(rng, dims, cuts, smallest, top_value):
    factor_of = 1.0
    for axis_at, parts in cuts:
        heights = jax.random.uniform(jax.random.fold_in(jax.random.fold_in(rng, 6), axis_at), (parts,), jnp.float32, smallest / len(cuts), top_value / len(cuts))
        factor_of = factor_of * jnp.repeat(jnp.exp(heights), dims[axis_at] // parts).reshape((-1,) + (1,) * (len(dims) - 1 - axis_at))
    return factor_of


def scatter_about(stream_key, extent, spread, bound, shards=(), held_as=jnp.bfloat16):
    level = steps_of(stream_key, extent, shards, -0.22, 0.18) if shards else 1.0
    values = jax.random.normal(stream_key, extent, jnp.float32) * spread * level
    return jnp.minimum(jnp.maximum(values, -bound), bound).astype(held_as)


def setup_inputs(seed: int = 0) -> dict:
    key_list = jax.random.split(jax.random.key(seed), 6)
    ensemble = scatter_about(key_list[0], (K, P_SIZE, S), 1.0, 6.0, ((0, 32),))
    obs_site = with_ends(jax.random.randint(key_list[1], (P_SIZE, BMAX * OB), 0, S), jax.random.fold_in(key_list[1], 1), 0, S - 1).astype(jnp.int32)
    obs_blocks = with_ends(jax.random.randint(key_list[2], (P_SIZE,), 1, BMAX + 1), jax.random.fold_in(key_list[2], 1), 1, BMAX).astype(jnp.int32)
    obs_precision = jnp.clip(jnp.exp(math.log(1.0) - 2.9996462 * jax.random.uniform(key_list[3], (P_SIZE, BMAX * OB), jnp.float32) ** steps_of(key_list[3], (P_SIZE, BMAX * OB), ((0, 32),), -0.2, 0.2)), 0.049804688, 1.0).astype(jnp.bfloat16)
    obs_innovation = scatter_about(key_list[4], (P_SIZE, BMAX * OB), 1.0, 6.0, ((0, 32),))
    return {"ensemble": ensemble, "obs_site": obs_site, "obs_blocks": obs_blocks, "obs_precision": obs_precision, "obs_innovation": obs_innovation}


def matmul_high(left, right):
    return jnp.matmul(left, right, precision=lax.Precision.HIGHEST)

def transform_weights(gram, rhs):
    members = gram.shape[-1]
    eye = jnp.eye(members, dtype=jnp.float32)
    amat = (members - 1.0) * eye + gram
    scale = jnp.sqrt(lax.optimization_barrier(jnp.sum(amat * amat, axis=(-2, -1))))[..., None, None]
    yk = amat / scale
    zk = jnp.broadcast_to(eye, amat.shape)
    for step in range(ITERS):
        tk = 1.5 * eye - 0.5 * matmul_high(zk, yk)
        yk = matmul_high(yk, tk)
        zk = matmul_high(tk, zk)
    wmean = matmul_high(zk, matmul_high(zk, rhs[..., None]))[..., 0] / scale[..., 0]
    coef = wmean[..., :, None] + jnp.sqrt(members - 1.0) * zk / jnp.sqrt(scale)
    return coef.astype(jnp.bfloat16)

def one_patch(items):
    member_rows, sites, blocks, precision, innovation = items
    values = member_rows.astype(jnp.float32)
    mean = lax.optimization_barrier(jnp.mean(values, axis=0))
    pert = (values - mean[None, :]).astype(jnp.bfloat16)
    slots = jnp.arange(sites.shape[0], dtype=jnp.int32) // OB
    live = jnp.where(slots < blocks, precision.astype(jnp.float32), jnp.float32(0.0))
    cols = jnp.take(pert, sites, axis=1)
    scaled = (cols.astype(jnp.float32) * live[None, :]).astype(jnp.bfloat16)
    gram = lax.dot_general(scaled, cols, (((1,), (1,)), ((), ())), preferred_element_type=jnp.float32)
    rhs = jnp.dot(scaled, innovation, preferred_element_type=jnp.float32)
    coef = transform_weights(gram, rhs)
    update = jnp.dot(coef.T, pert, preferred_element_type=jnp.float32)
    return (mean[None, :] + update).astype(jnp.bfloat16)

def reference(ensemble, obs_site, obs_blocks, obs_precision, obs_innovation):
    by_patch = jnp.transpose(ensemble, (1, 0, 2))
    result = lax.map(one_patch, (by_patch, obs_site, obs_blocks, obs_precision, obs_innovation))
    return jnp.transpose(result, (1, 0, 2))
```

```python
import functools
import math

import jax
import jax.numpy as jnp
from jax import lax
from jax.experimental import pallas as pl
from jax.experimental.pallas import tpu as pltpu
from jax.sharding import PartitionSpec as P

OB = 128
ITERS = 6
LANES = 128
VMEM = pl.BlockSpec(memory_space=pltpu.VMEM)
SMEM = pl.BlockSpec(memory_space=pltpu.SMEM)
F32 = jnp.float32
BF16 = jnp.bfloat16
PARAMS = pltpu.CompilerParams(vmem_limit_bytes=40 * 2**20)


def cost(flops, touched):
    return pl.CostEstimate(flops=flops, bytes_accessed=touched, transcendentals=0)


def dot(left, right):
    return lax.dot_general(left, right, (((1,), (0,)), ((), ())), preferred_element_type=F32)


def dot_rows(left, right):
    return lax.dot_general(left, right, (((1,), (1,)), ((), ())), preferred_element_type=F32)


def split(value):
    high = value.astype(BF16)
    return high, (value - high.astype(F32)).astype(BF16)


def dot_split(left, right):
    return dot(left[0], right[0]) + (dot(left[0], right[1]) + dot(left[1], right[0]))


def site_sums_kernel(states, blocks_ref, site_ref, precision_ref, innovation_ref, weight_ref, value_ref):
    patches, slots = site_ref.shape
    groups = states // LANES
    rows = lax.broadcasted_iota(jnp.int32, (groups, slots), 0)
    lanes = lax.broadcasted_iota(jnp.int32, (LANES, slots), 0)
    slot = lax.broadcasted_iota(jnp.int32, (1, slots), 1)
    for patch in range(patches):
        sites = site_ref[patch : patch + 1, :]
        alive = slot < blocks_ref[patch] * OB
        live = jnp.where(alive, precision_ref[patch : patch + 1, :].astype(F32), 0.0)
        value = live * innovation_ref[patch : patch + 1, :].astype(F32)
        high = value.astype(BF16).astype(F32)
        picked = rows == sites // LANES
        left = jnp.concatenate(
            [jnp.where(picked, part, 0.0) for part in (live, high, value - high)], axis=0
        ).astype(BF16)
        right = jnp.where(lanes == sites % LANES, 1.0, 0.0).astype(BF16)
        sums = dot_rows(left, right)
        for group in range(groups):
            columns = slice(group * LANES, (group + 1) * LANES)
            weight_ref[patch : patch + 1, columns] = sums[group : group + 1]
            value_ref[patch : patch + 1, columns] = (
                sums[groups + group : groups + group + 1]
                + sums[2 * groups + group : 2 * groups + group + 1]
            )


def analyse_kernel(first, senders, weight_ref, value_ref, *refs):
    ins, outs = refs[:senders], refs[senders:]
    patches, part, states = ins[0].shape
    members = senders * part
    grid_rows = lax.broadcasted_iota(jnp.int32, (members, members), 0)
    grid_columns = lax.broadcasted_iota(jnp.int32, (members, members), 1)
    eye = jnp.where(grid_rows == grid_columns, 1.0, 0.0)
    every = range(patches)

    means, perts, rests, scales, sides = [], [], [], [], []
    for patch in every:
        total = sum(jnp.sum(ref[patch].astype(F32), axis=0, keepdims=True) for ref in ins)
        mean = total / members
        pert = jnp.concatenate([(ref[patch].astype(F32) - mean).astype(BF16) for ref in ins], axis=0)
        weight = weight_ref[first + patch : first + patch + 1, :]
        value = value_ref[first + patch : first + patch + 1, :]
        scaled = split(pert.astype(F32) * weight)
        gram = dot_rows(scaled[0], pert) + dot_rows(scaled[1], pert)
        sides.append(
            dot_rows(jnp.concatenate([jnp.broadcast_to(part_, (8, states)) for part_ in split(value)], axis=0), pert)
        )
        amat = (members - 1.0) * eye + gram
        square = jnp.sum(jnp.sum(amat * amat, axis=1, keepdims=True), axis=0, keepdims=True)
        scale = lax.rsqrt(square)
        means.append(mean)
        perts.append(pert)
        scales.append(scale)
        rests.append(eye - amat * scale)

    zs = [eye + 0.5 * rest for rest in rests]
    for step in range(1, ITERS):
        parts = [split(rest) for rest in rests]
        squares = [dot_split(part_, part_) for part_ in parts]
        halves = [split(square) for square in squares]
        rests = [
            0.75 * square + 0.25 * dot_split(half, part_)
            for square, half, part_ in zip(squares, halves, parts)
        ]
        zs = [z + 0.5 * dot_split(split(rest), split(z)) for rest, z in zip(rests, zs)]

    for patch in every:
        z = split(zs[patch])
        row = sides[patch][0:1] + sides[patch][8:9]
        for _ in range(2):
            high, low = split(jnp.broadcast_to(row, (8, members)))
            row = (dot(high, z[0]) + (dot(high, z[1]) + dot(low, z[0])))[0:1]
        wmean = row * scales[patch]
        coef = wmean + (math.sqrt(members - 1.0) * lax.sqrt(scales[patch])) * zs[patch]
        update = dot(coef.astype(BF16), perts[patch])
        result = (means[patch] + update).astype(BF16)
        for sender, ref in enumerate(outs):
            ref[patch] = result[sender * part : (sender + 1) * part]


def pack_kernel(first, count, regions, place_ref, ensemble_ref, *outs):
    held = ensemble_ref.shape[1] // (len(outs) * regions)
    for k, out in enumerate(outs):
        def region(j, carry):
            owner = (place_ref[0] ^ k) * regions + (place_ref[1] ^ j)
            rows = pl.ds(pl.multiple_of(owner * held, held), held)
            block = ensemble_ref[:, rows, :].astype(F32)[:, first : first + count, :]
            out[j] = jnp.swapaxes(block, 0, 1).astype(BF16)
            return carry

        lax.fori_loop(0, regions, region, 0)


def turn_kernel(*refs, ins):
    sources, outs = refs[:ins], refs[ins:]
    members = sources[0].shape[2]
    for j, out in enumerate(outs):
        for patch in range(out.shape[0]):
            out[patch] = jnp.concatenate([source[j, patch] for source in sources], axis=0)


def unturn_kernel(*refs, ins):
    sources, outs = refs[:ins], refs[ins:]
    members = outs[0].shape[2]
    for j, source in enumerate(sources):
        for patch in range(source.shape[0]):
            for k, out in enumerate(outs):
                out[j, patch] = source[patch, k * members : (k + 1) * members, :]


def unpack_kernel(chunks, regions, partners, place_ref, *refs):
    sources, out = refs[:-1], refs[-1]
    held = out.shape[1] // (partners * regions)
    for k in range(partners):
        def region(j, carry):
            owner = (place_ref[0] ^ k) * regions + (place_ref[1] ^ j)
            rows = pl.ds(pl.multiple_of(owner * held, held), held)
            block = jnp.concatenate(
                [sources[chunk * partners + k][j].astype(F32) for chunk in range(chunks)], axis=0
            )
            out[:, rows, :] = jnp.swapaxes(block, 0, 1).astype(BF16)
            return carry

        lax.fori_loop(0, regions, region, 0)


def exchange(blocks, axis):
    size = len(blocks)
    return [blocks[0]] + [
        lax.ppermute(blocks[k], axis, [(i, i ^ k) for i in range(size)]) for k in range(1, size)
    ]


def local(partners, regions, ensemble, obs_site, obs_blocks, obs_precision, obs_innovation):
    members, patches, states = ensemble.shape
    held = obs_site.shape[0]
    chunks = 4
    count = held // chunks
    place = jnp.stack([lax.axis_index("member"), lax.axis_index("region")]).astype(jnp.int32)
    total = members * partners * regions
    sums = jax.ShapeDtypeStruct((held, states), F32)
    z_block = jax.ShapeDtypeStruct((regions, count, members, states), BF16)
    r_block = jax.ShapeDtypeStruct((count, partners * members, states), BF16)
    chunk_bytes = 2 * count * total * states

    packed = [
        pl.pallas_call(
            functools.partial(pack_kernel, chunk * count, count, regions),
            out_shape=[z_block] * partners,
            in_specs=[SMEM, VMEM],
            out_specs=[VMEM] * partners,
            compiler_params=PARAMS,
            cost_estimate=cost(0, 2 * chunk_bytes),
            name="pack",
        )(place, ensemble)
        for chunk in range(chunks)
    ]
    weight, value = pl.pallas_call(
        functools.partial(site_sums_kernel, states),
        out_shape=[sums, sums],
        in_specs=[SMEM, VMEM, VMEM, VMEM],
        out_specs=[VMEM, VMEM],
        compiler_params=PARAMS,
        cost_estimate=cost(2 * held * 16 * 2048 * 128, 8 * held * 2048),
        name="site_sums",
    )(obs_blocks, obs_site, obs_precision, obs_innovation)

    finished = []
    for chunk in range(chunks):
        arrived = exchange(packed[chunk], "member")
        turned = pl.pallas_call(
            functools.partial(turn_kernel, ins=partners),
            out_shape=[r_block] * regions,
            in_specs=[VMEM] * partners,
            out_specs=[VMEM] * regions,
            compiler_params=PARAMS,
            cost_estimate=cost(0, 2 * chunk_bytes),
            name="turn",
        )(*arrived)
        gathered = exchange(turned, "region")
        analysed = pl.pallas_call(
            functools.partial(analyse_kernel, chunk * count, regions),
            out_shape=[r_block] * regions,
            in_specs=[VMEM] * (2 + regions),
            out_specs=[VMEM] * regions,
            compiler_params=PARAMS,
            cost_estimate=cost(count * 51 * 2 * total**3, 2 * chunk_bytes),
            name="analyse",
        )(weight, value, *gathered)
        back = exchange(analysed, "region")
        unturned = pl.pallas_call(
            functools.partial(unturn_kernel, ins=regions),
            out_shape=[z_block] * partners,
            in_specs=[VMEM] * regions,
            out_specs=[VMEM] * partners,
            compiler_params=PARAMS,
            cost_estimate=cost(0, 2 * chunk_bytes),
            name="unturn",
        )(*back)
        finished += exchange(unturned, "member")
    return pl.pallas_call(
        functools.partial(unpack_kernel, chunks, regions, partners),
        out_shape=jax.ShapeDtypeStruct(ensemble.shape, BF16),
        in_specs=[SMEM] + [VMEM] * len(finished),
        out_specs=VMEM,
        compiler_params=PARAMS,
        cost_estimate=cost(0, 2 * chunk_bytes * chunks),
        name="unpack",
    )(place, *finished)


def solution(mesh):
    placed = (
        P(("member", "region"), None, None),
        P(("member", "region"), None),
        P(("member", "region")),
        P(("member", "region"), None),
        P(("member", "region"), None),
    )
    return jax.shard_map(
        functools.partial(local, mesh.shape["member"], mesh.shape["region"]),
        mesh=mesh,
        in_specs=placed,
        out_specs=P(("member", "region"), None, None),
        check_vma=False,
    )
```

```python
import functools
import math

import jax
import jax.numpy as jnp
from jax import lax
from jax.experimental import pallas as pl
from jax.experimental.pallas import tpu as pltpu
from jax.sharding import PartitionSpec as P

OB = 128
ITERS = 6
LANES = 128
LONG = 10**11
VMEM = pl.BlockSpec(memory_space=pltpu.VMEM)
ANY = pl.BlockSpec(memory_space=pl.ANY)
SMEM = pl.BlockSpec(memory_space=pltpu.SMEM)
F32 = jnp.float32
BF16 = jnp.bfloat16
PARAMS = pltpu.CompilerParams(vmem_limit_bytes=40 * 2**20)


def cost(flops, touched):
    return pl.CostEstimate(flops=flops, bytes_accessed=touched, transcendentals=0)


def dot(left, right):
    return lax.dot_general(left, right, (((1,), (0,)), ((), ())), preferred_element_type=F32)


def dot_rows(left, right):
    return lax.dot_general(left, right, (((1,), (1,)), ((), ())), preferred_element_type=F32)


def split(value):
    high = value.astype(BF16)
    return high, (value - high.astype(F32)).astype(BF16)


def dot_split(left, right):
    return dot(
        jnp.concatenate([left[0], left[0], left[1]], axis=1),
        jnp.concatenate([right[0], right[1], right[0]], axis=0),
    )


def site_sums_kernel(states, blocks_ref, site_ref, precision_ref, innovation_ref, *refs):
    weight_ref, value_ref = refs[-2:]
    patches, slots = site_ref.shape
    groups = states // LANES
    rows = lax.broadcasted_iota(jnp.int32, (groups, slots), 0)
    lanes = lax.broadcasted_iota(jnp.int32, (LANES, slots), 0)
    slot = lax.broadcasted_iota(jnp.int32, (1, slots), 1)
    for patch in range(patches):
        sites = site_ref[patch : patch + 1, :]
        alive = slot < blocks_ref[patch] * OB
        live = jnp.where(alive, precision_ref[patch : patch + 1, :].astype(F32), 0.0)
        value = live * innovation_ref[patch : patch + 1, :].astype(F32)
        high = value.astype(BF16).astype(F32)
        picked = rows == sites // LANES
        left = jnp.concatenate(
            [jnp.where(picked, part, 0.0) for part in (live, high, value - high)], axis=0
        ).astype(BF16)
        right = jnp.where(lanes == sites % LANES, 1.0, 0.0).astype(BF16)
        sums = dot_rows(left, right)
        for group in range(groups):
            columns = slice(group * LANES, (group + 1) * LANES)
            weight_ref[patch : patch + 1, columns] = sums[group : group + 1]
            value_ref[patch : patch + 1, columns] = (
                sums[groups + group : groups + group + 1]
                + sums[2 * groups + group : 2 * groups + group + 1]
            )


def views(refs, size):
    return [refs[0].at[i] for i in range(size)] if len(refs) == 1 else list(refs)


def analyse_kernel(first, senders, receivers, taken, given, weight_ref, value_ref, *refs):
    ins, outs = views(refs[:taken], senders), views(refs[-given:], receivers)
    patches, part, states = ins[0].shape
    members = senders * part
    block = part // receivers
    grid_rows = lax.broadcasted_iota(jnp.int32, (members, members), 0)
    grid_columns = lax.broadcasted_iota(jnp.int32, (members, members), 1)
    eye = jnp.where(grid_rows == grid_columns, 1.0, 0.0)
    every = range(patches)

    means, perts, rests, scales, sides = [], [], [], [], []
    for patch in every:
        total = sum(jnp.sum(ref[patch].astype(F32), axis=0, keepdims=True) for ref in ins)
        mean = total / members
        pert = jnp.concatenate([(ref[patch].astype(F32) - mean).astype(BF16) for ref in ins], axis=0)
        weight = weight_ref[first + patch : first + patch + 1, :]
        value = value_ref[first + patch : first + patch + 1, :]
        scaled = split(pert.astype(F32) * weight)
        gram = dot_rows(jnp.concatenate(scaled, axis=1), jnp.concatenate([pert, pert], axis=1))
        sides.append(
            dot_rows(jnp.concatenate([jnp.broadcast_to(part_, (8, states)) for part_ in split(value)], axis=0), pert)
        )
        amat = (members - 1.0) * eye + gram
        square = jnp.sum(jnp.sum(amat * amat, axis=0, keepdims=True), axis=1, keepdims=True)
        scale = lax.rsqrt(square)
        means.append(mean)
        perts.append(pert)
        scales.append(scale)
        rests.append(eye - amat * scale)

    zs = [eye + 0.5 * rest for rest in rests]
    parts = [split(rest) for rest in rests]
    for step in range(1, ITERS):
        squares = [dot_split(part_, part_) for part_ in parts]
        halves = [split(0.25 * square) for square in squares]
        rests = [
            0.75 * square + dot_split(half, part_) for square, half, part_ in zip(squares, halves, parts)
        ]
        parts = [split(rest) for rest in rests]
        zs = [z + 0.5 * dot_split(part_, split(z)) for part_, z in zip(parts, zs)]

    for patch in every:
        z = split(zs[patch])
        row = sides[patch][0:1] + sides[patch][8:9]
        for _ in range(2):
            high, low = split(jnp.broadcast_to(row, (8, members)))
            row = (dot(high, z[0]) + (dot(high, z[1]) + dot(low, z[0])))[0:1]
        wmean = row * scales[patch]
        coef = wmean + (math.sqrt(members - 1.0) * lax.sqrt(scales[patch])) * zs[patch]
        update = dot(coef.astype(BF16), perts[patch])
        result = (means[patch] + update).astype(BF16)
        for sender in range(senders):
            for k, out in enumerate(outs):
                row_at = sender * part + k * block
                out[sender, patch] = result[row_at : row_at + block]


def pack_kernel(first, flip, seconds, firsts, given, place_ref, ensemble_ref, *refs):
    outs = views(refs[-given:], firsts)
    count = outs[0].shape[1]
    held = ensemble_ref.shape[1] // (firsts * seconds)
    regions = firsts if flip else seconds
    for f, out in enumerate(outs):
        def second(g, carry):
            k, j = (g, f) if flip else (f, g)
            owner = (place_ref[0] ^ k) * regions + j
            rows = pl.ds(pl.multiple_of(owner * held, held), held)
            block = ensemble_ref[:, rows, :].astype(F32)[:, first : first + count, :]
            out[g] = jnp.swapaxes(block, 0, 1).astype(BF16)
            return carry

        lax.fori_loop(0, seconds, second, 0)


def turn_kernel(firsts, seconds, taken, given, *refs):
    sources, outs = views(refs[:taken], firsts), views(refs[-given:], seconds)
    for g, out in enumerate(outs):
        for patch in range(out.shape[0]):
            out[patch] = jnp.concatenate([source[g, patch] for source in sources], axis=0)


def unpack_kernel(flips, regions, partners, place_ref, *refs):
    out = refs[-1]
    members = out.shape[0]
    held = out.shape[1] // (partners * regions)
    sources, at = [], 0
    for flip in flips:
        size = partners if flip else regions
        taken = partners if flip else 1
        sources.append(views(refs[at : at + taken], size))
        at += taken
    for k in range(partners):
        for j in range(regions):
            owner = (place_ref[0] ^ k) * regions + j
            rows = pl.ds(pl.multiple_of(owner * held, held), held)
            pieces = []
            for flip, arrays in zip(flips, sources):
                f, g = (j, k) if flip else (k, j)
                pieces.append(arrays[g][:, f * members : (f + 1) * members, :].astype(F32))
            out[:, rows, :] = jnp.swapaxes(jnp.concatenate(pieces, axis=0), 0, 1).astype(BF16)


def hold_kernel(*refs):
    refs[-1][...] = jnp.zeros_like(refs[-1])


def exchange(blocks, axis):
    if axis == "region":
        return [lax.all_to_all(blocks[0], axis, split_axis=0, concat_axis=0, tiled=True)]
    size = len(blocks)
    return [blocks[0]] + [
        lax.ppermute(blocks[k], axis, [(i, i ^ k) for i in range(size)]) for k in range(1, size)
    ]


def local(partners, regions, ensemble, obs_site, obs_blocks, obs_precision, obs_innovation):
    members, _, states = ensemble.shape
    held = obs_site.shape[0]
    place = lax.axis_index("member").astype(jnp.int32)[None]
    total = members * partners * regions
    flips = [False, True]
    counts = [held // 2, held - held // 2]
    starts = [0, held // 2]
    axes = [("member", "region"), ("region", "member")]
    sizes = [(partners, regions), (regions, partners)]
    last = [[]]
    state = {}

    def run(kernel, name, shapes, scalars, arrays, flops=0, touched=0):
        result = pl.pallas_call(
            kernel,
            out_shape=shapes,
            in_specs=[SMEM] * len(scalars) + [VMEM] * len(arrays) + [ANY] * len(last[0]),
            out_specs=[VMEM] * len(shapes),
            compiler_params=PARAMS,
            cost_estimate=cost(flops, touched),
            name=name,
        )(*scalars, *arrays, *last[0])
        last[0] = [result[0]]
        return result

    def blocks(axis, size, *shape):
        if axis == "region":
            return [jax.ShapeDtypeStruct((size,) + shape + (states,), BF16)]
        return [jax.ShapeDtypeStruct(shape + (states,), BF16)] * size

    def site_sums():
        sums = jax.ShapeDtypeStruct((held, states), F32)
        state["sums"] = run(
            functools.partial(site_sums_kernel, states), "site_sums", [sums, sums], [obs_blocks],
            [obs_site, obs_precision, obs_innovation],
        )

    def pack(c):
        first, second = sizes[c]
        shapes = blocks(axes[c][0], first, second, counts[c], members)
        packed = run(
            functools.partial(pack_kernel, starts[c], flips[c], second, first, len(shapes)), "pack",
            shapes, [place], [ensemble],
        )
        state[c] = exchange(packed, axes[c][0])

    def turn(c, flops=0):
        first, second = sizes[c]
        shapes = blocks(axes[c][1], second, counts[c], first * members)
        turned = run(
            functools.partial(turn_kernel, first, second, len(state[c]), len(shapes)), "turn",
            shapes, [], state[c], flops,
        )
        state[c] = exchange(turned, axes[c][1])

    def analyse(c):
        first, second = sizes[c]
        shapes = blocks(axes[c][0], first, second, counts[c], members)
        analysed = run(
            functools.partial(analyse_kernel, starts[c], second, first, len(state[c]), len(shapes)), "analyse",
            shapes, [], list(state["sums"]) + state[c],
            0,
        )
        state[c] = exchange(analysed, axes[c][0])

    def hold(c, flops):
        last[0] = last[0] + state[c]
        run(hold_kernel, "hold", [jax.ShapeDtypeStruct((8, LANES), F32)], [], [], flops)

    pack(0)
    pack(1)
    site_sums()
    turn(0, LONG)
    turn(1)
    analyse(0)
    analyse(1)
    turn(0, LONG)
    turn(1)
    hold(1, LONG)
    return run(
        functools.partial(unpack_kernel, flips, regions, partners), "unpack",
        [jax.ShapeDtypeStruct(ensemble.shape, BF16)], [place], state[0] + state[1],
    )[0]


def solution(mesh):
    placed = (
        P(("member", "region"), None, None),
        P(("member", "region"), None),
        P(("member", "region")),
        P(("member", "region"), None),
        P(("member", "region"), None),
    )
    return jax.shard_map(
        functools.partial(local, mesh.shape["member"], mesh.shape["region"]),
        mesh=mesh,
        in_specs=placed,
        out_specs=P(("member", "region"), None, None),
        check_vma=False,
    )
```

```python
import functools
import math

import jax
import jax.numpy as jnp
from jax import lax
from jax.experimental import pallas as pl
from jax.experimental.pallas import tpu as pltpu
from jax.sharding import PartitionSpec as P

OB = 128
ITERS = 6
LANES = 128
LONG = 10**11
SHORT = 10**10
VMEM = pl.BlockSpec(memory_space=pltpu.VMEM)
ANY = pl.BlockSpec(memory_space=pl.ANY)
SMEM = pl.BlockSpec(memory_space=pltpu.SMEM)
F32 = jnp.float32
BF16 = jnp.bfloat16
PARAMS = pltpu.CompilerParams(vmem_limit_bytes=40 * 2**20)


def cost(flops, touched):
    return pl.CostEstimate(flops=flops, bytes_accessed=touched, transcendentals=0)


def dot(left, right):
    return lax.dot_general(left, right, (((1,), (0,)), ((), ())), preferred_element_type=F32)


def dot_rows(left, right):
    return lax.dot_general(left, right, (((1,), (1,)), ((), ())), preferred_element_type=F32)


def split(value):
    high = value.astype(BF16)
    return high, (value - high.astype(F32)).astype(BF16)


def dot_split(left, right):
    return dot(
        jnp.concatenate([left[0], left[0], left[1]], axis=1),
        jnp.concatenate([right[0], right[1], right[0]], axis=0),
    )


def site_sums_kernel(states, blocks_ref, site_ref, precision_ref, innovation_ref, *refs):
    weight_ref, value_ref = refs[-2:]
    patches, slots = site_ref.shape
    groups = states // LANES
    rows = lax.broadcasted_iota(jnp.int32, (groups, slots), 0)
    lanes = lax.broadcasted_iota(jnp.int32, (LANES, slots), 0)
    slot = lax.broadcasted_iota(jnp.int32, (1, slots), 1)
    for patch in range(patches):
        sites = site_ref[patch : patch + 1, :]
        alive = slot < blocks_ref[patch] * OB
        live = jnp.where(alive, precision_ref[patch : patch + 1, :].astype(F32), 0.0)
        value = live * innovation_ref[patch : patch + 1, :].astype(F32)
        high = value.astype(BF16).astype(F32)
        picked = rows == sites // LANES
        left = jnp.concatenate(
            [jnp.where(picked, part, 0.0) for part in (live, high, value - high)], axis=0
        ).astype(BF16)
        right = jnp.where(lanes == sites % LANES, 1.0, 0.0).astype(BF16)
        sums = dot_rows(left, right)
        for group in range(groups):
            columns = slice(group * LANES, (group + 1) * LANES)
            weight_ref[patch : patch + 1, columns] = sums[group : group + 1]
            value_ref[patch : patch + 1, columns] = (
                sums[groups + group : groups + group + 1]
                + sums[2 * groups + group : 2 * groups + group + 1]
            )


def views(refs, size):
    return [refs[0].at[i] for i in range(size)] if len(refs) == 1 else list(refs)


def analyse_kernel(first, senders, taken, weight_ref, value_ref, *refs):
    ins, outs = views(refs[:taken], senders), views(refs[-taken:], senders)
    patches, part, states = ins[0].shape
    members = senders * part
    blocks = outs[0].shape[0]
    block = part // blocks
    grid_rows = lax.broadcasted_iota(jnp.int32, (members, members), 0)
    grid_columns = lax.broadcasted_iota(jnp.int32, (members, members), 1)
    eye = jnp.where(grid_rows == grid_columns, 1.0, 0.0)
    every = range(patches)

    means, perts, rests, scales, sides = [], [], [], [], []
    for patch in every:
        total = sum(jnp.sum(ref[patch].astype(F32), axis=0, keepdims=True) for ref in ins)
        mean = total / members
        pert = jnp.concatenate([(ref[patch].astype(F32) - mean).astype(BF16) for ref in ins], axis=0)
        weight = weight_ref[first + patch : first + patch + 1, :]
        value = value_ref[first + patch : first + patch + 1, :]
        wide = pert.astype(F32)
        scaled = split(wide * weight)
        gram = dot_rows(jnp.concatenate(scaled, axis=1), jnp.concatenate([pert, pert], axis=1))
        sides.append(jnp.sum(wide * value, axis=1, keepdims=True))
        amat = (members - 1.0) * eye + gram
        square = jnp.sum(jnp.sum(amat * amat, axis=0, keepdims=True), axis=1, keepdims=True)
        scale = lax.rsqrt(square)
        means.append(mean)
        perts.append(pert)
        scales.append(scale)
        rests.append(eye - amat * scale)

    zs = [eye + 0.5 * rest for rest in rests]
    parts = [split(rest) for rest in rests]
    for step in range(1, ITERS):
        squares = [dot_split(part_, part_) for part_ in parts]
        halves = [split(0.25 * square) for square in squares]
        rests = [
            0.75 * square + dot_split(half, part_) for square, half, part_ in zip(squares, halves, parts)
        ]
        parts = [split(rest) for rest in rests]
        zs = [z + 0.5 * dot_split(part_, split(z)) for part_, z in zip(parts, zs)]

    for patch in every:
        z = split(zs[patch])
        row = split(jnp.broadcast_to(jnp.sum(sides[patch] * zs[patch], axis=0, keepdims=True), (8, members)))
        both = dot(jnp.concatenate(row, axis=0), z[0])
        wmean = (both[0:1] + (both[8:9] + dot(row[0], z[1])[0:1])) * scales[patch]
        coef = wmean + (math.sqrt(members - 1.0) * lax.sqrt(scales[patch])) * zs[patch]
        update = dot(coef.astype(BF16), perts[patch])
        result = (means[patch] + update).astype(BF16)
        for sender, out in enumerate(outs):
            for k in range(blocks):
                row_at = sender * part + k * block
                out[k, patch] = result[row_at : row_at + block]


def pack_kernel(first, flip, seconds, firsts, given, place_ref, ensemble_ref, *refs):
    outs = views(refs[-given:], firsts)
    count = outs[0].shape[1]
    held = ensemble_ref.shape[1] // (firsts * seconds)
    regions = firsts if flip else seconds
    for f, out in enumerate(outs):
        def second(g, carry):
            k, j = (g, f) if flip else (f, g)
            owner = (place_ref[0] ^ k) * regions + j
            rows = pl.ds(pl.multiple_of(owner * held, held), held)
            block = ensemble_ref[:, rows, :].astype(F32)[:, first : first + count, :]
            out[g] = jnp.swapaxes(block, 0, 1).astype(BF16)
            return carry

        lax.fori_loop(0, seconds, second, 0)


def turn_kernel(first, firsts, seconds, groups, taken, given, *refs):
    outs = views(refs[-given:], seconds)
    at = 0
    for group in range(groups):
        sources = views(refs[group * taken : (group + 1) * taken], firsts)
        count = min(sources[0].shape[1] - first, outs[0].shape[0])
        for g, out in enumerate(outs):
            for patch in range(count):
                out[at + patch] = jnp.concatenate([source[g, first + patch] for source in sources], axis=0)
        at += count


def unpack_kernel(flips, regions, partners, place_ref, *refs):
    out = refs[-1]
    members = out.shape[0]
    held = out.shape[1] // (partners * regions)
    sources, at = [], 0
    for flip in flips:
        size = partners if flip else regions
        taken = partners if flip else 1
        sources.append(views(refs[at : at + taken], size))
        at += taken
    for k in range(partners):
        for j in range(regions):
            owner = (place_ref[0] ^ k) * regions + j
            rows = pl.ds(pl.multiple_of(owner * held, held), held)
            pieces = []
            for flip, arrays in zip(flips, sources):
                f, g = (j, k) if flip else (k, j)
                pieces.append(arrays[g][:, f * members : (f + 1) * members, :].astype(F32))
            out[:, rows, :] = jnp.swapaxes(jnp.concatenate(pieces, axis=0), 0, 1).astype(BF16)


def hold_kernel(*refs):
    refs[-1][...] = jnp.zeros_like(refs[-1])


def exchange(blocks, axis):
    if axis == "region":
        return [lax.all_to_all(blocks[0], axis, split_axis=0, concat_axis=0, tiled=True)]
    size = len(blocks)
    return [blocks[0]] + [
        lax.ppermute(blocks[k], axis, [(i, i ^ k) for i in range(size)]) for k in range(1, size)
    ]


def local(partners, regions, ensemble, obs_site, obs_blocks, obs_precision, obs_innovation):
    members, _, states = ensemble.shape
    held = obs_site.shape[0]
    place = lax.axis_index("member").astype(jnp.int32)[None]
    total = members * partners * regions
    y_count = held // 2
    x_counts = [(held - y_count) // 2, held - y_count - (held - y_count) // 2]
    x_count = sum(x_counts)
    sizes = {"member": partners, "region": regions}
    last = [[]]
    state = {}

    def run(kernel, name, shapes, scalars, arrays, flops=0, touched=0):
        result = pl.pallas_call(
            kernel,
            out_shape=shapes,
            in_specs=[SMEM] * len(scalars) + [VMEM] * len(arrays) + [ANY] * len(last[0]),
            out_specs=[VMEM] * len(shapes),
            compiler_params=PARAMS,
            cost_estimate=cost(flops, touched),
            name=name,
        )(*scalars, *arrays, *last[0])
        last[0] = [result[0]]
        return result

    def blocks(axis, size, *shape):
        if axis == "region":
            return [jax.ShapeDtypeStruct((size,) + shape + (states,), BF16)]
        return [jax.ShapeDtypeStruct(shape + (states,), BF16)] * size

    def site_sums():
        sums = jax.ShapeDtypeStruct((held, states), F32)
        state["sums"] = run(
            functools.partial(site_sums_kernel, states), "site_sums", [sums, sums], [obs_blocks],
            [obs_site, obs_precision, obs_innovation],
        )

    def pack(c, first, count, axis, other):
        shapes = blocks(axis, sizes[axis], sizes[other], count, members)
        packed = run(
            functools.partial(pack_kernel, first, axis == "region", sizes[other], sizes[axis], len(shapes)),
            "pack", shapes, [place], [ensemble],
        )
        state[c] = exchange(packed, axis)

    def turn(c, sources, first, count, axis, other, flops=0):
        arrays = [array for source in sources for array in state[source]]
        shapes = blocks(other, sizes[other], count, sizes[axis] * members)
        turned = run(
            functools.partial(
                turn_kernel, first, sizes[axis], sizes[other], len(sources),
                len(arrays) // len(sources), len(shapes),
            ),
            "turn", shapes, [], arrays, flops,
        )
        state[c] = exchange(turned, other)

    def analyse(c, first, count, axis, other, flops=0):
        shapes = blocks(axis, sizes[axis], sizes[other], count, members)
        analysed = run(
            functools.partial(analyse_kernel, first, sizes[axis], len(shapes)), "analyse",
            shapes, [], list(state["sums"]) + state[c], flops,
        )
        state[c] = exchange(analysed, axis)

    def hold(arrays, flops):
        last[0] = last[0] + list(arrays)
        run(hold_kernel, "hold", [jax.ShapeDtypeStruct((8, LANES), F32)], [], [], flops)

    pack("y", 0, y_count, "member", "region")
    pack("x", y_count, x_count, "region", "member")
    site_sums()
    hold(state["y"][1:-1], LONG)
    turn("x0", ["x"], 0, x_counts[0], "region", "member")
    turn("y", ["y"], 0, y_count, "member", "region", LONG)
    turn("x1", ["x"], x_counts[0], x_counts[1], "region", "member")
    analyse("x0", y_count, x_counts[0], "member", "region", LONG)
    analyse("y", 0, y_count, "region", "member")
    analyse("x1", y_count + x_counts[0], x_counts[1], "member", "region")
    hold(state["x0"], SHORT)
    turn("y", ["y"], 0, y_count, "region", "member")
    turn("x", ["x0", "x1"], 0, x_count, "member", "region", LONG)
    hold(state["y"], LONG)
    return run(
        functools.partial(unpack_kernel, [True, False], regions, partners), "unpack",
        [jax.ShapeDtypeStruct(ensemble.shape, BF16)], [place], state["y"] + state["x"],
    )[0]


def solution(mesh):
    placed = (
        P(("member", "region"), None, None),
        P(("member", "region"), None),
        P(("member", "region")),
        P(("member", "region"), None),
        P(("member", "region"), None),
    )
    return jax.shard_map(
        functools.partial(local, mesh.shape["member"], mesh.shape["region"]),
        mesh=mesh,
        in_specs=placed,
        out_specs=P(("member", "region"), None, None),
        check_vma=False,
    )
```

```python
import functools
import math

import jax
import jax.numpy as jnp
from jax import lax
from jax.experimental import pallas as pl
from jax.experimental.pallas import tpu as pltpu
from jax.sharding import PartitionSpec as P

OB = 128
ITERS = 6
LANES = 128
LONG = 10**11
SHORT = 10**10
VMEM = pl.BlockSpec(memory_space=pltpu.VMEM)
ANY = pl.BlockSpec(memory_space=pl.ANY)
SMEM = pl.BlockSpec(memory_space=pltpu.SMEM)
F32 = jnp.float32
BF16 = jnp.bfloat16
PARAMS = pltpu.CompilerParams(vmem_limit_bytes=40 * 2**20)


def cost(flops, touched):
    return pl.CostEstimate(flops=flops, bytes_accessed=touched, transcendentals=0)


def dot(left, right):
    return lax.dot_general(left, right, (((1,), (0,)), ((), ())), preferred_element_type=F32)


def dot_rows(left, right):
    return lax.dot_general(left, right, (((1,), (1,)), ((), ())), preferred_element_type=F32)


def split(value):
    high = value.astype(BF16)
    return high, (value - high.astype(F32)).astype(BF16)


def dot_split(left, right):
    return dot(
        jnp.concatenate([left[0], left[0], left[1]], axis=1),
        jnp.concatenate([right[0], right[1], right[0]], axis=0),
    )


def dot_stacked(lefts, right):
    rows = sum(left[0].shape[0] for left in lefts)
    highs = [left[0] for left in lefts]
    main = dot(jnp.concatenate(highs + [left[1] for left in lefts], axis=0), right[0])
    rest = dot(jnp.concatenate(highs, axis=0), right[1]) if len(highs) > 1 else dot(highs[0], right[1])
    return main[:rows] + (main[rows:] + rest)


def site_sums_kernel(states, blocks_ref, site_ref, precision_ref, innovation_ref, *refs):
    weight_ref, value_ref = refs[-2:]
    patches, slots = site_ref.shape
    groups = states // LANES
    rows = lax.broadcasted_iota(jnp.int32, (groups, slots), 0)
    lanes = lax.broadcasted_iota(jnp.int32, (LANES, slots), 0)
    slot = lax.broadcasted_iota(jnp.int32, (1, slots), 1)
    for patch in range(patches):
        sites = site_ref[patch : patch + 1, :]
        alive = slot < blocks_ref[patch] * OB
        live = jnp.where(alive, precision_ref[patch : patch + 1, :].astype(F32), 0.0)
        value = live * innovation_ref[patch : patch + 1, :].astype(F32)
        high = value.astype(BF16).astype(F32)
        picked = rows == sites // LANES
        left = jnp.concatenate(
            [jnp.where(picked, part, 0.0) for part in (live, high, value - high)], axis=0
        ).astype(BF16)
        right = jnp.where(lanes == sites % LANES, 1.0, 0.0).astype(BF16)
        sums = dot_rows(left, right)
        for group in range(groups):
            columns = slice(group * LANES, (group + 1) * LANES)
            weight_ref[patch : patch + 1, columns] = sums[group : group + 1]
            value_ref[patch : patch + 1, columns] = (
                sums[groups + group : groups + group + 1]
                + sums[2 * groups + group : 2 * groups + group + 1]
            )


def views(refs, size):
    return [refs[0].at[i] for i in range(size)] if len(refs) == 1 else list(refs)


def analyse_kernel(first, senders, taken, weight_ref, value_ref, *refs):
    ins, outs = views(refs[:taken], senders), views(refs[-taken:], senders)
    patches, part, states = ins[0].shape
    members = senders * part
    blocks = outs[0].shape[0]
    block = part // blocks
    grid_rows = lax.broadcasted_iota(jnp.int32, (members, members), 0)
    grid_columns = lax.broadcasted_iota(jnp.int32, (members, members), 1)
    eye = jnp.where(grid_rows == grid_columns, 1.0, 0.0)
    every = range(patches)

    means, perts, rests, scales, sides = [], [], [], [], []
    for patch in every:
        total = sum(jnp.sum(ref[patch].astype(F32), axis=0, keepdims=True) for ref in ins)
        mean = total / members
        pert = jnp.concatenate([(ref[patch].astype(F32) - mean).astype(BF16) for ref in ins], axis=0)
        weight = weight_ref[first + patch : first + patch + 1, :]
        value = value_ref[first + patch : first + patch + 1, :]
        wide = pert.astype(F32)
        scaled = split(wide * weight)
        gram = dot_rows(jnp.concatenate(scaled, axis=1), jnp.concatenate([pert, pert], axis=1))
        sides.append(jnp.sum(wide * value, axis=1, keepdims=True))
        amat = (members - 1.0) * eye + gram
        square = jnp.sum(jnp.sum(amat * amat, axis=0, keepdims=True), axis=1, keepdims=True)
        scale = lax.rsqrt(square)
        means.append(mean)
        perts.append(pert)
        scales.append(scale)
        rests.append(eye - amat * scale)

    zs = [eye + 0.5 * rest for rest in rests]
    for step in range(1, ITERS):
        parts = [split(rest) for rest in rests]
        if step == 1:
            squares = [dot_split(part_, part_) for part_ in parts]
        else:
            both = [dot_stacked([part_, split(z)], part_) for part_, z in zip(parts, zs)]
            squares = [pair[:members] for pair in both]
            zs = [z + 0.5 * pair[members:] for z, pair in zip(zs, both)]
        rests = [
            0.75 * square + dot_stacked([split(0.25 * square)], part_) for square, part_ in zip(squares, parts)
        ]
    zs = [z + 0.5 * dot_split(split(z), split(rest)) for rest, z in zip(rests, zs)]

    for patch in every:
        z = split(zs[patch])
        row = split(jnp.broadcast_to(jnp.sum(sides[patch] * zs[patch], axis=0, keepdims=True), (8, members)))
        both = dot(jnp.concatenate(row, axis=0), z[0])
        wmean = (both[0:1] + (both[8:9] + dot(row[0], z[1])[0:1])) * scales[patch]
        coef = wmean + (math.sqrt(members - 1.0) * lax.sqrt(scales[patch])) * zs[patch]
        update = dot(coef.astype(BF16), perts[patch])
        result = (means[patch] + update).astype(BF16)
        for sender, out in enumerate(outs):
            for k in range(blocks):
                row_at = sender * part + k * block
                out[k, patch] = result[row_at : row_at + block]


def pack_kernel(first, flip, seconds, firsts, given, place_ref, ensemble_ref, *refs):
    outs = views(refs[-given:], firsts)
    count = outs[0].shape[1]
    held = ensemble_ref.shape[1] // (firsts * seconds)
    regions = firsts if flip else seconds
    for f, out in enumerate(outs):
        def second(g, carry):
            k, j = (g, f) if flip else (f, g)
            owner = (place_ref[0] ^ k) * regions + j
            rows = pl.ds(pl.multiple_of(owner * held, held), held)
            block = ensemble_ref[:, rows, :].astype(F32)[:, first : first + count, :]
            out[g] = jnp.swapaxes(block, 0, 1).astype(BF16)
            return carry

        lax.fori_loop(0, seconds, second, 0)


def turn_kernel(first, firsts, seconds, groups, taken, given, *refs):
    outs = views(refs[-given:], seconds)
    at = 0
    for group in range(groups):
        sources = views(refs[group * taken : (group + 1) * taken], firsts)
        count = min(sources[0].shape[1] - first, outs[0].shape[0])
        for g, out in enumerate(outs):
            for patch in range(count):
                out[at + patch] = jnp.concatenate([source[g, first + patch] for source in sources], axis=0)
        at += count


def unpack_kernel(flips, regions, partners, place_ref, *refs):
    out = refs[-1]
    members = out.shape[0]
    held = out.shape[1] // (partners * regions)
    sources, at = [], 0
    for flip in flips:
        size = partners if flip else regions
        taken = partners if flip else 1
        sources.append(views(refs[at : at + taken], size))
        at += taken
    for k in range(partners):
        for j in range(regions):
            owner = (place_ref[0] ^ k) * regions + j
            rows = pl.ds(pl.multiple_of(owner * held, held), held)
            pieces = []
            for flip, arrays in zip(flips, sources):
                f, g = (j, k) if flip else (k, j)
                pieces.append(arrays[g][:, f * members : (f + 1) * members, :].astype(F32))
            out[:, rows, :] = jnp.swapaxes(jnp.concatenate(pieces, axis=0), 0, 1).astype(BF16)


def hold_kernel(*refs):
    refs[-1][...] = jnp.zeros_like(refs[-1])


def exchange(blocks, axis):
    if axis == "region":
        return [lax.all_to_all(blocks[0], axis, split_axis=0, concat_axis=0, tiled=True)]
    size = len(blocks)
    return [blocks[0]] + [
        lax.ppermute(blocks[k], axis, [(i, i ^ k) for i in range(size)]) for k in range(1, size)
    ]


def local(partners, regions, ensemble, obs_site, obs_blocks, obs_precision, obs_innovation):
    members, _, states = ensemble.shape
    held = obs_site.shape[0]
    place = lax.axis_index("member").astype(jnp.int32)[None]
    total = members * partners * regions
    y_count = held // 2
    x_counts = [(held - y_count) // 2, held - y_count - (held - y_count) // 2]
    x_count = sum(x_counts)
    sizes = {"member": partners, "region": regions}
    last = [[]]
    state = {}

    def run(kernel, name, shapes, scalars, arrays, flops=0, touched=0):
        result = pl.pallas_call(
            kernel,
            out_shape=shapes,
            in_specs=[SMEM] * len(scalars) + [VMEM] * len(arrays) + [ANY] * len(last[0]),
            out_specs=[VMEM] * len(shapes),
            compiler_params=PARAMS,
            cost_estimate=cost(flops, touched),
            name=name,
        )(*scalars, *arrays, *last[0])
        last[0] = [result[0]]
        return result

    def blocks(axis, size, *shape):
        if axis == "region":
            return [jax.ShapeDtypeStruct((size,) + shape + (states,), BF16)]
        return [jax.ShapeDtypeStruct(shape + (states,), BF16)] * size

    def site_sums():
        sums = jax.ShapeDtypeStruct((held, states), F32)
        state["sums"] = run(
            functools.partial(site_sums_kernel, states), "site_sums", [sums, sums], [obs_blocks],
            [obs_site, obs_precision, obs_innovation],
        )

    def pack(c, first, count, axis, other):
        shapes = blocks(axis, sizes[axis], sizes[other], count, members)
        packed = run(
            functools.partial(pack_kernel, first, axis == "region", sizes[other], sizes[axis], len(shapes)),
            "pack", shapes, [place], [ensemble],
        )
        state[c] = exchange(packed, axis)

    def turn(c, sources, first, count, axis, other, flops=0):
        arrays = [array for source in sources for array in state[source]]
        shapes = blocks(other, sizes[other], count, sizes[axis] * members)
        turned = run(
            functools.partial(
                turn_kernel, first, sizes[axis], sizes[other], len(sources),
                len(arrays) // len(sources), len(shapes),
            ),
            "turn", shapes, [], arrays, flops,
        )
        state[c] = exchange(turned, other)

    def analyse(c, first, count, axis, other, flops=0):
        shapes = blocks(axis, sizes[axis], sizes[other], count, members)
        analysed = run(
            functools.partial(analyse_kernel, first, sizes[axis], len(shapes)), "analyse",
            shapes, [], list(state["sums"]) + state[c], flops,
        )
        state[c] = exchange(analysed, axis)

    def hold(arrays, flops):
        last[0] = last[0] + list(arrays)
        run(hold_kernel, "hold", [jax.ShapeDtypeStruct((8, LANES), F32)], [], [], flops)

    pack("y", 0, y_count, "member", "region")
    pack("x", y_count, x_count, "region", "member")
    site_sums()
    hold(state["y"][1:-1], LONG)
    turn("x0", ["x"], 0, x_counts[0], "region", "member")
    turn("y", ["y"], 0, y_count, "member", "region", LONG)
    turn("x1", ["x"], x_counts[0], x_counts[1], "region", "member")
    analyse("x0", y_count, x_counts[0], "member", "region", LONG)
    analyse("y", 0, y_count, "region", "member")
    analyse("x1", y_count + x_counts[0], x_counts[1], "member", "region")
    hold(state["x0"], SHORT)
    turn("y", ["y"], 0, y_count, "region", "member")
    turn("x", ["x0", "x1"], 0, x_count, "member", "region", LONG)
    hold(state["y"], LONG)
    return run(
        functools.partial(unpack_kernel, [True, False], regions, partners), "unpack",
        [jax.ShapeDtypeStruct(ensemble.shape, BF16)], [place], state["y"] + state["x"],
    )[0]


def solution(mesh):
    placed = (
        P(("member", "region"), None, None),
        P(("member", "region"), None),
        P(("member", "region")),
        P(("member", "region"), None),
        P(("member", "region"), None),
    )
    return jax.shard_map(
        functools.partial(local, mesh.shape["member"], mesh.shape["region"]),
        mesh=mesh,
        in_specs=placed,
        out_specs=P(("member", "region"), None, None),
        check_vma=False,
    )
```
